32 devices in a mesh: frame: 8 (over z, x), slab: 4 (over y, core).
Axes of the slice: x: 2, y: 2, z: 4, core: 2. Of those that a mesh axis runs over, the one named last changes fastest.
Arguments:
- latents: bfloat16 [16, 16, 160, 512], P('frame', 'slab'), may hold values from -20 to 20
- clip_starts: int32 [16], replicated, may hold values from 0 to 1
- w_space: bfloat16 [3, 3, 512, 512], replicated, may hold values from -0.09375 to 0.09375
- w_time: bfloat16 [3, 512, 512], replicated, may hold values from -0.15625 to 0.15625
- w_qkv: bfloat16 [512, 1536], replicated, may hold values from -0.25 to 0.25
- w_out: bfloat16 [512, 512], replicated, may hold values from -0.25 to 0.25
Outputs:
- block_out: bfloat16 [16, 16, 160, 512], P('frame', 'slab')
The draws below stay inside these ranges and needn't reach their ends.
All inputs are finite; a program needn't handle non-finite values.
Results may differ from the reference program's by a relative error of at most 0.0065.
Values may be sent and summed in bfloat16 or wider, within the bound.
A program may use at most 64 MiB of HBM per device.

```python
import math
import jax
import jax.numpy as jnp
from jax import lax

C = 512
HEADS = 8
WIDTH = 160
FRAMES = 16
HEIGHT = 16


def draw_latents(key, part):
    key_one = jax.random.fold_in(jax.random.fold_in(key, 11), 0)
    values = jnp.clip(jax.random.normal(key_one, (FRAMES, HEIGHT, WIDTH, C), jnp.float32), -6.0, 6.0)
    return values.astype(jnp.bfloat16)


def draw_clip_starts(key, part):
    picked = jax.random.randint(jax.random.fold_in(key, 23), (FRAMES,), 0, 20)
    flagged = (picked == 0).astype(jnp.int32)
    return flagged.at[0].set(1)


def gaussian(own_key, dims, deviation, most, kind=jnp.bfloat16):
    return jnp.clip(deviation * jax.random.normal(own_key, dims, jnp.float32), -most, most).astype(kind)


def setup_inputs(seed: int = 0) -> dict:
    key_of = jax.random.split(jax.random.key(seed), 7)
    return {
        "latents": draw_latents(jax.random.fold_in(key_of[6], 71), 0),
        "clip_starts": draw_clip_starts(jax.random.fold_in(key_of[6], 71), 0),
        "w_space": gaussian(key_of[2], (3, 3, C, C), (9 * C) ** -0.5, 0.09375),
        "w_time": gaussian(key_of[3], (3, C, C), (3 * C) ** -0.5, 0.15625),
        "w_qkv": gaussian(key_of[4], (C, 3 * C), C ** -0.5, 0.25),
        "w_out": gaussian(key_of[5], (C, C), C ** -0.5, 0.25),
    }


def space_conv(padded_rows, w_space):
    frames, rows_padded, columns, channels = padded_rows.shape
    row_count = rows_padded - 2
    widened = jnp.pad(padded_rows, ((0, 0), (0, 0), (1, 1), (0, 0)))
    summed = jnp.zeros((frames * row_count * columns, channels), jnp.float32)
    for row_shift in range(3):
        for col_shift in range(3):
            source = widened[:, row_shift:row_shift + row_count, col_shift:col_shift + columns].reshape(-1, channels)
            summed = summed + jnp.dot(source, w_space[row_shift, col_shift], preferred_element_type=jnp.float32)
    return jax.nn.silu(summed).astype(jnp.bfloat16).reshape(frames, row_count, columns, channels)

def clip_window(clip_starts, first_frame, count):
    clip_ids = jnp.cumsum(clip_starts).astype(jnp.int32)
    padded = jnp.concatenate([jnp.full((2,), -1, jnp.int32), clip_ids])
    return lax.dynamic_slice_in_dim(padded, first_frame, count + 2)

def time_conv(extended, window, w_time):
    count = extended.shape[0] - 2
    middle = extended.shape[1:-1]
    channels = extended.shape[-1]
    summed = jnp.zeros((count,) + middle + (channels,), jnp.float32)
    for offset in range(3):
        source = extended[2 - offset:2 - offset + count].reshape(-1, channels)
        product = jnp.dot(source, w_time[offset], preferred_element_type=jnp.float32).reshape((count,) + middle + (channels,))
        allowed = (window[2 - offset:2 - offset + count] == window[2:]).astype(jnp.float32)
        summed = summed + product * allowed.reshape((count,) + (1,) * (len(middle) + 1))
    return summed.astype(jnp.bfloat16)

def project(mixed_in, w_qkv):
    frames, pixels, channels = mixed_in.shape
    flattened = jnp.dot(mixed_in.reshape(-1, channels), w_qkv, preferred_element_type=jnp.float32)
    queries = flattened[:, :channels].astype(jnp.bfloat16).reshape(frames, pixels, channels)
    keys_out = flattened[:, channels:2 * channels].astype(jnp.bfloat16).reshape(frames, pixels, channels)
    values = flattened[:, 2 * channels:].astype(jnp.bfloat16).reshape(frames, pixels, channels)
    return (queries, keys_out, values)

def attend(queries, keys_in, values, allowed, head_count):
    frames, pixels, channels = queries.shape
    head_size = channels // head_count
    query_f = queries.reshape(frames, pixels, head_count, head_size).astype(jnp.float32)
    key_f = keys_in.reshape(frames, pixels, head_count, head_size).astype(jnp.float32)
    value_f = values.reshape(frames, pixels, head_count, head_size).astype(jnp.float32)
    scores = jnp.einsum('iphd,jphd->phij', query_f, key_f) * (1.0 / math.sqrt(head_size))
    scores = jnp.where(allowed, scores, -1e+30)
    weights = jax.nn.softmax(scores, axis=-1).astype(jnp.bfloat16)
    attended = jnp.einsum('phij,jphd->iphd', weights.astype(jnp.float32), value_f)
    return attended.reshape(frames, pixels, channels).astype(jnp.bfloat16)

def reference(latents, clip_starts, w_space, w_time, w_qkv, w_out):
    total_frames, height, columns, channels = latents.shape

    def one_frame(frame_data):
        return space_conv(jnp.pad(frame_data, ((1, 1), (0, 0), (0, 0)))[None], w_space)[0]
    hidden = lax.map(one_frame, latents)
    window = clip_window(clip_starts, 0, total_frames)
    extended = jnp.concatenate([jnp.zeros((2, height, columns, channels), hidden.dtype), hidden])
    mixed_in = time_conv(extended, window, w_time)
    clip_ids = window[2:]
    positions = jnp.arange(total_frames)
    allowed = (positions[None, :] <= positions[:, None]) & (clip_ids[None, :] == clip_ids[:, None])

    def per_row(row_data):
        queries, keys_out, values = project(row_data, w_qkv)
        attended = attend(queries, keys_out, values, allowed, HEADS)
        return jnp.dot(attended.reshape(-1, channels), w_out, preferred_element_type=jnp.float32).astype(jnp.bfloat16).reshape(total_frames, columns, channels)
    att_out = jnp.moveaxis(lax.map(per_row, jnp.moveaxis(mixed_in, 1, 0)), 0, 1)
    return (latents.astype(jnp.float32) + att_out.astype(jnp.float32)).astype(jnp.bfloat16)
```

```python
import functools
import math

import jax
import jax.numpy as jnp
from jax import lax
from jax.experimental import pallas as pl
from jax.experimental.pallas import tpu as pltpu
from jax.sharding import PartitionSpec as P

HEADS = 8
BLOCK = 16
SHIFT = 4
MESH = pl.DeviceIdType.MESH


def with_halo(block, sides, width):
    for axis, dim in sides:
        count = lax.axis_size(axis)
        forward = [(i, i + 1) for i in range(count - 1)]
        backward = [(target, source) for source, target in forward]
        low = lax.ppermute(
            lax.slice_in_dim(block, block.shape[dim] - width, None, axis=dim), axis, forward
        )
        high = lax.ppermute(lax.slice_in_dim(block, 0, width, axis=dim), axis, backward)
        block = jnp.concatenate([low, block, high], axis=dim)
    return block


def space_conv(padded_rows, w_space):
    frames, rows_padded, columns, channels = padded_rows.shape
    row_count = rows_padded - 2
    widened = jnp.pad(padded_rows, ((0, 0), (0, 0), (1, 1), (0, 0)))
    summed = jnp.zeros((frames * row_count * columns, channels), jnp.float32)
    for row_shift in range(3):
        for col_shift in range(3):
            source = widened[
                :, row_shift : row_shift + row_count, col_shift : col_shift + columns
            ].reshape(-1, channels)
            summed = summed + jnp.dot(
                source, w_space[row_shift, col_shift], preferred_element_type=jnp.float32
            )
    return jax.nn.silu(summed).astype(jnp.bfloat16).reshape(frames, row_count, columns, channels)


def clip_window(clip_starts):
    positions = jnp.arange(clip_starts.shape[0])
    upto = positions[None, :] <= positions[:, None]
    clip_ids = jnp.sum(jnp.where(upto, clip_starts[None, :], 0), axis=1)
    return jnp.concatenate([jnp.full((2,), -1, jnp.int32), clip_ids])


def time_conv(extended, window, w_time):
    count = extended.shape[0] - 2
    middle = extended.shape[1:-1]
    channels = extended.shape[-1]
    summed = jnp.zeros((count,) + middle + (channels,), jnp.float32)
    for offset in range(3):
        source = extended[2 - offset : 2 - offset + count].reshape(-1, channels)
        product = jnp.dot(source, w_time[offset], preferred_element_type=jnp.float32).reshape(
            (count,) + middle + (channels,)
        )
        allowed = (window[2 - offset : 2 - offset + count] == window[2:]).astype(jnp.float32)
        summed = summed + product * allowed.reshape((count,) + (1,) * (len(middle) + 1))
    return summed.astype(jnp.bfloat16)


def project(mixed_in, w_qkv):
    frames, pixels, channels = mixed_in.shape
    flattened = jnp.dot(mixed_in.reshape(-1, channels), w_qkv, preferred_element_type=jnp.float32)
    flattened = flattened.astype(jnp.bfloat16).reshape(frames, pixels, 3 * channels)
    return (
        flattened[..., :channels],
        flattened[..., channels : 2 * channels],
        flattened[..., 2 * channels :],
    )


def attend(queries, keys_in, values, allowed, head_count):
    frames, pixels, channels = queries.shape
    head_size = channels // head_count
    query_f = queries.reshape(frames, pixels, head_count, head_size).astype(jnp.float32)
    key_f = keys_in.reshape(frames, pixels, head_count, head_size).astype(jnp.float32)
    value_f = values.reshape(frames, pixels, head_count, head_size).astype(jnp.float32)
    scores = jnp.einsum("iphd,jphd->phij", query_f, key_f) * (1.0 / math.sqrt(head_size))
    scores = jnp.where(allowed, scores, -1e30)
    weights = jax.nn.softmax(scores, axis=-1).astype(jnp.bfloat16)
    attended = jnp.einsum("phij,jphd->iphd", weights.astype(jnp.float32), value_f)
    return attended.reshape(frames, pixels, channels).astype(jnp.bfloat16)


def general(latents, clip_starts, w_space, w_time, w_qkv, w_out):
    frames, row_count, columns, channels = latents.shape
    device_count = lax.axis_size("frame")
    total_frames = clip_starts.shape[0]
    owned = row_count * columns // device_count
    padded = with_halo(latents, (("slab", 1),), 1)
    hidden = space_conv(padded, w_space)
    full_window = clip_window(clip_starts)
    clip_ids = full_window[2:]
    positions = jnp.arange(total_frames)
    allowed = (positions[None, :] <= positions[:, None]) & (clip_ids[None, :] == clip_ids[:, None])
    payload = hidden.reshape(frames, device_count, owned, channels)
    arrived = lax.all_to_all(payload, "frame", split_axis=1, concat_axis=0, tiled=True)
    pixels = arrived.shape[2]
    extended = jnp.concatenate([jnp.zeros((2, 1, pixels, channels), arrived.dtype), arrived])
    arrived = time_conv(extended, full_window, w_time)
    flattened = arrived.reshape(total_frames, pixels, channels)
    queries, keys_out, values = project(flattened, w_qkv)
    attended = attend(queries, keys_out, values, allowed, HEADS)
    result = jnp.dot(attended.reshape(-1, channels), w_out, preferred_element_type=jnp.float32)
    result = result.astype(jnp.bfloat16).reshape(total_frames, 1, pixels, channels)
    returned = lax.all_to_all(result, "frame", split_axis=0, concat_axis=1, tiled=True)
    returned = returned.reshape(frames, row_count, columns, channels)
    return (latents.astype(jnp.float32) + returned.astype(jnp.float32)).astype(jnp.bfloat16)


def kernel(
    n, slabs, row_count, columns, head_count,
    lat_hbm, starts, ws_hbm, wt_hbm, wqkv_hbm, wo_hbm, out_ref,
    x, ws, wt, wqkv, wo, hid, rx, tx, ret, bias, lag_mask, att,
    load_sem, halo_send, halo_recv, fwd_send, fwd_recv, back_send, back_recv,
):
    frames, pixels, channels = lat_hbm.shape
    total = n * frames
    rows = total * BLOCK
    chunks = pixels // (BLOCK * n)
    blocks = pixels // BLOCK
    first = columns // BLOCK
    me = lax.axis_index("frame")
    slab = lax.axis_index("slab")
    up, down = lax.rem(slab + 1, slabs), lax.rem(slab + slabs - 1, slabs)

    barrier = pltpu.get_barrier_semaphore()
    for step in range(1, n):
        pl.semaphore_signal(
            barrier, inc=1, device_id=(lax.rem(me + step, n), slab), device_id_type=MESH
        )
    for other in (up, down):
        pl.semaphore_signal(barrier, inc=1, device_id=(me, other), device_id_type=MESH)

    loads = [
        pltpu.make_async_copy(source, target, load_sem.at[i])
        for i, (source, target) in enumerate(
            (
                (lat_hbm, x.at[:, columns : columns + pixels]),
                (ws_hbm, ws),
                (wt_hbm, wt),
                (wqkv_hbm, wqkv),
                (wo_hbm, wo),
            )
        )
    ]
    for load in loads:
        load.start()

    pl.semaphore_wait(barrier, n + 1)
    halos = [
        pltpu.make_async_remote_copy(
            src_ref=lat_hbm.at[:, pixels - columns : pixels],
            dst_ref=x.at[:, 0:columns],
            send_sem=halo_send.at[0],
            recv_sem=halo_recv.at[0],
            device_id=(me, up),
            device_id_type=MESH,
        ),
        pltpu.make_async_remote_copy(
            src_ref=lat_hbm.at[:, 0:columns],
            dst_ref=x.at[:, columns + pixels : 2 * columns + pixels],
            send_sem=halo_send.at[1],
            recv_sem=halo_recv.at[1],
            device_id=(me, down),
            device_id_type=MESH,
        ),
    ]
    for halo in halos:
        halo.start()

    ids = []
    for f in range(total):
        ids.append(starts[f] if f == 0 else ids[-1] + starts[f])
    row = lax.broadcasted_iota(jnp.int32, (rows, 1), 0)
    col = lax.broadcasted_iota(jnp.int32, (1, rows), 1)
    row_frame, row_pixel = lax.shift_right_logical(row, SHIFT), row & (BLOCK - 1)
    col_frame, col_pixel = lax.shift_right_logical(col, SHIFT), col & (BLOCK - 1)
    row_id, col_id = jnp.zeros_like(row), jnp.zeros_like(col)
    lags = [jnp.zeros((rows, 1), jnp.float32) for _ in range(2)]
    for f in range(total):
        row_id = jnp.where(row_frame == f, ids[f], row_id)
        col_id = jnp.where(col_frame == f, ids[f], col_id)
        for lag in (1, 2):
            if f >= lag:
                same = jnp.where(ids[f - lag] == ids[f], 1.0, 0.0)
                lags[lag - 1] = jnp.where(row_frame == f, same, lags[lag - 1])
    allowed = (row_pixel == col_pixel) & (col_frame <= row_frame) & (row_id == col_id)
    bias[...] = jnp.where(allowed, 0.0, -1e30)
    for lag in range(2):
        lag_mask[lag] = jnp.broadcast_to(lags[lag], (rows, channels)).astype(jnp.bfloat16)

    def conv_row(r):
        sums = []
        for b in range(3):
            total_b = None
            for a in range(3):
                source = x[:, pl.ds(pl.multiple_of((r + a) * columns, BLOCK), columns), :]
                part = jnp.dot(
                    source.reshape(frames * columns, channels),
                    ws[a, b],
                    preferred_element_type=jnp.float32,
                )
                total_b = part if total_b is None else total_b + part
            sums.append(total_b)
        place = lax.broadcasted_iota(jnp.int32, (columns, channels), 0)
        for f in range(frames):
            part = [s[f * columns : (f + 1) * columns] for s in sums]
            left = jnp.where(place == 0, 0.0, pltpu.roll(part[0], 1, 0))
            right = jnp.where(place == columns - 1, 0.0, pltpu.roll(part[2], columns - 1, 0))
            v = part[1] + left + right
            hid[f, pl.ds(pl.multiple_of(r * columns, BLOCK), columns), :] = (
                v / (1.0 + jnp.exp(-v))
            ).astype(jnp.bfloat16)

    def spot(k, owner):
        return pl.multiple_of(lax.rem(first + n * k + owner, blocks) * BLOCK, BLOCK)

    def forward(k, step):
        peer = lax.rem(me + step, n)
        return pltpu.make_async_remote_copy(
            src_ref=hid.at[:, pl.ds(spot(k, peer), BLOCK), :],
            dst_ref=rx.at[k, pl.ds(me * frames, frames)],
            send_sem=fwd_send.at[k, step],
            recv_sem=fwd_recv.at[k, step],
            device_id=(peer, slab),
            device_id_type=MESH,
        )

    def backward(k, step):
        peer = lax.rem(me + step, n)
        return pltpu.make_async_remote_copy(
            src_ref=tx.at[k, pl.ds(peer * frames, frames)],
            dst_ref=ret.at[:, pl.ds(spot(k, me), BLOCK), :],
            send_sem=back_send.at[k, step],
            recv_sem=back_recv.at[k, step],
            device_id=(peer, slab),
            device_id_type=MESH,
        )

    def send_forward(k):
        for step in range(1, n):
            forward(k, step).start()
        rx[k, pl.ds(me * frames, frames)] = hid[:, pl.ds(spot(k, me), BLOCK), :]

    inner = (row_count - 2) * columns // (BLOCK * n)
    loads[0].wait()
    loads[1].wait()

    @pl.loop(0, row_count - 2)
    def _(t):
        conv_row(t + 1)

    for k in range(inner):
        send_forward(k)
    for halo in halos:
        halo.wait()

    @pl.when(slab == 0)
    def _():
        x[:, 0:columns] = jnp.zeros((frames, columns, channels), jnp.bfloat16)

    @pl.when(slab == slabs - 1)
    def _():
        x[:, columns + pixels : 2 * columns + pixels] = jnp.zeros(
            (frames, columns, channels), jnp.bfloat16
        )

    @pl.loop(0, 2)
    def _(t):
        conv_row((1 - t) * (row_count - 1))

    @pl.loop(inner, chunks)
    def _(k):
        send_forward(k)

    for load in loads[2:]:
        load.wait()

    lanes = 2 * (channels // head_count)
    low = lax.broadcasted_iota(jnp.int32, (rows, lanes), 1) < lanes // 2
    scale = 1.0 / math.sqrt(channels // head_count)

    @pl.loop(0, chunks)
    def _(k):
        for step in range(1, n):
            forward(k, step).wait_recv()
        own = rx[k].reshape(rows, channels)
        mixed = jnp.dot(own, wt[0], preferred_element_type=jnp.float32)
        for lag in (1, 2):
            gap = lag * BLOCK
            lagged = jnp.concatenate(
                [jnp.zeros((gap, channels), jnp.bfloat16), own[: rows - gap]], axis=0
            )
            mixed = mixed + jnp.dot(
                lagged * lag_mask[lag - 1], wt[lag], preferred_element_type=jnp.float32
            )
        mixed = mixed.astype(jnp.bfloat16)
        for pair in range(channels // lanes):
            q, key, value = (
                jnp.dot(
                    mixed,
                    wqkv[:, third * channels + pair * lanes : third * channels + (pair + 1) * lanes],
                    preferred_element_type=jnp.float32,
                ).astype(jnp.bfloat16)
                for third in range(3)
            )
            outs = []
            for half in range(2):
                mine = low if half == 0 else jnp.logical_not(low)
                q_half = jnp.where(mine, q, jnp.zeros_like(q))
                s = lax.dot_general(
                    q_half, key, (((1,), (1,)), ((), ())), preferred_element_type=jnp.float32
                )
                s = s * scale + bias[...]
                e = jnp.exp(s - jnp.max(s, axis=1, keepdims=True))
                norm = jnp.sum(e, axis=1, keepdims=True)
                o = jnp.dot(e.astype(jnp.bfloat16), value, preferred_element_type=jnp.float32)
                outs.append(o / norm)
            att[:, pair * lanes : (pair + 1) * lanes] = jnp.where(low, outs[0], outs[1]).astype(
                jnp.bfloat16
            )
        result = jnp.dot(att[...], wo[...], preferred_element_type=jnp.float32)
        tx[k] = result.astype(jnp.bfloat16).reshape(total, BLOCK, channels)
        for step in range(1, n):
            backward(k, step).start()
        ret[:, pl.ds(spot(k, me), BLOCK), :] = tx[k, pl.ds(me * frames, frames)]

    @pl.loop(0, chunks)
    def _(k):
        for step in range(1, n):
            backward(k, step).wait_recv()
        for owner in range(n):
            here = spot(k, owner)
            moved = x[:, pl.ds(here + columns, BLOCK), :].astype(jnp.float32)
            moved = moved + ret[:, pl.ds(here, BLOCK), :].astype(jnp.float32)
            out_ref[:, pl.ds(here, BLOCK), :] = moved.astype(jnp.bfloat16)

    @pl.loop(0, chunks)
    def _(k):
        for step in range(1, n):
            forward(k, step).wait_send()
            backward(k, step).wait_send()


def fused(latents, clip_starts, w_space, w_time, w_qkv, w_out):
    frames, row_count, columns, channels = latents.shape
    n, slabs = lax.axis_size("frame"), lax.axis_size("slab")
    pixels = row_count * columns
    total = clip_starts.shape[0]
    chunks = pixels // (BLOCK * n)
    rows = total * BLOCK
    bf16 = jnp.bfloat16
    out = pl.pallas_call(
        functools.partial(kernel, n, slabs, row_count, columns, HEADS),
        out_shape=jax.ShapeDtypeStruct((frames, pixels, channels), bf16),
        in_specs=[
            pl.BlockSpec(memory_space=pl.ANY),
            pl.BlockSpec(memory_space=pltpu.SMEM),
        ]
        + [pl.BlockSpec(memory_space=pl.ANY)] * 4,
        out_specs=pl.BlockSpec(memory_space=pltpu.VMEM),
        scratch_shapes=[
            pltpu.VMEM((frames, pixels + 2 * columns, channels), bf16),
            pltpu.VMEM(w_space.shape, bf16),
            pltpu.VMEM(w_time.shape, bf16),
            pltpu.VMEM(w_qkv.shape, bf16),
            pltpu.VMEM(w_out.shape, bf16),
            pltpu.VMEM((frames, pixels, channels), bf16),
            pltpu.VMEM((chunks, total, BLOCK, channels), bf16),
            pltpu.VMEM((chunks, total, BLOCK, channels), bf16),
            pltpu.VMEM((frames, pixels, channels), bf16),
            pltpu.VMEM((rows, rows), jnp.float32),
            pltpu.VMEM((2, rows, channels), bf16),
            pltpu.VMEM((rows, channels), bf16),
            pltpu.SemaphoreType.DMA((5,)),
            pltpu.SemaphoreType.DMA((2,)),
            pltpu.SemaphoreType.DMA((2,)),
            pltpu.SemaphoreType.DMA((chunks, n)),
            pltpu.SemaphoreType.DMA((chunks, n)),
            pltpu.SemaphoreType.DMA((chunks, n)),
            pltpu.SemaphoreType.DMA((chunks, n)),
        ],
        compiler_params=pltpu.CompilerParams(
            collective_id=0, has_side_effects=True, vmem_limit_bytes=40 * 2**20
        ),
    )(latents.reshape(frames, pixels, channels), clip_starts, w_space, w_time, w_qkv, w_out)
    return out.reshape(latents.shape)


def on_device(latents, clip_starts, w_space, w_time, w_qkv, w_out):
    frames, row_count, columns, channels = latents.shape
    n, slabs = lax.axis_size("frame"), lax.axis_size("slab")
    fits = (
        (row_count * columns) % (BLOCK * n) == 0
        and columns % BLOCK == 0
        and clip_starts.shape[0] * BLOCK <= 512
        and slabs >= 3
        and row_count >= 3
        and n >= 2
    )
    plan = fused if fits else general
    return plan(latents, clip_starts, w_space, w_time, w_qkv, w_out)


def solution(mesh):
    return jax.shard_map(
        on_device,
        mesh=mesh,
        in_specs=(P("frame", "slab", None, None), P(), P(), P(), P(), P()),
        out_specs=P("frame", "slab", None, None),
        check_vma=False,
    )
```

```python
import functools
import math

import jax
import jax.numpy as jnp
from jax import lax
from jax.experimental import pallas as pl
from jax.experimental.pallas import tpu as pltpu
from jax.sharding import PartitionSpec as P

HEADS = 8
BLOCK = 16
SHIFT = 4
MESH = pl.DeviceIdType.MESH


def with_halo(block, sides, width):
    for axis, dim in sides:
        count = lax.axis_size(axis)
        forward = [(i, i + 1) for i in range(count - 1)]
        backward = [(target, source) for source, target in forward]
        low = lax.ppermute(
            lax.slice_in_dim(block, block.shape[dim] - width, None, axis=dim), axis, forward
        )
        high = lax.ppermute(lax.slice_in_dim(block, 0, width, axis=dim), axis, backward)
        block = jnp.concatenate([low, block, high], axis=dim)
    return block


def space_conv(padded_rows, w_space):
    frames, rows_padded, columns, channels = padded_rows.shape
    row_count = rows_padded - 2
    widened = jnp.pad(padded_rows, ((0, 0), (0, 0), (1, 1), (0, 0)))
    summed = jnp.zeros((frames * row_count * columns, channels), jnp.float32)
    for row_shift in range(3):
        for col_shift in range(3):
            source = widened[
                :, row_shift : row_shift + row_count, col_shift : col_shift + columns
            ].reshape(-1, channels)
            summed = summed + jnp.dot(
                source, w_space[row_shift, col_shift], preferred_element_type=jnp.float32
            )
    return jax.nn.silu(summed).astype(jnp.bfloat16).reshape(frames, row_count, columns, channels)


def clip_window(clip_starts):
    positions = jnp.arange(clip_starts.shape[0])
    upto = positions[None, :] <= positions[:, None]
    clip_ids = jnp.sum(jnp.where(upto, clip_starts[None, :], 0), axis=1)
    return jnp.concatenate([jnp.full((2,), -1, jnp.int32), clip_ids])


def time_conv(extended, window, w_time):
    count = extended.shape[0] - 2
    middle = extended.shape[1:-1]
    channels = extended.shape[-1]
    summed = jnp.zeros((count,) + middle + (channels,), jnp.float32)
    for offset in range(3):
        source = extended[2 - offset : 2 - offset + count].reshape(-1, channels)
        product = jnp.dot(source, w_time[offset], preferred_element_type=jnp.float32).reshape(
            (count,) + middle + (channels,)
        )
        allowed = (window[2 - offset : 2 - offset + count] == window[2:]).astype(jnp.float32)
        summed = summed + product * allowed.reshape((count,) + (1,) * (len(middle) + 1))
    return summed.astype(jnp.bfloat16)


def project(mixed_in, w_qkv):
    frames, pixels, channels = mixed_in.shape
    flattened = jnp.dot(mixed_in.reshape(-1, channels), w_qkv, preferred_element_type=jnp.float32)
    flattened = flattened.astype(jnp.bfloat16).reshape(frames, pixels, 3 * channels)
    return (
        flattened[..., :channels],
        flattened[..., channels : 2 * channels],
        flattened[..., 2 * channels :],
    )


def attend(queries, keys_in, values, allowed, head_count):
    frames, pixels, channels = queries.shape
    head_size = channels // head_count
    query_f = queries.reshape(frames, pixels, head_count, head_size).astype(jnp.float32)
    key_f = keys_in.reshape(frames, pixels, head_count, head_size).astype(jnp.float32)
    value_f = values.reshape(frames, pixels, head_count, head_size).astype(jnp.float32)
    scores = jnp.einsum("iphd,jphd->phij", query_f, key_f) * (1.0 / math.sqrt(head_size))
    scores = jnp.where(allowed, scores, -1e30)
    weights = jax.nn.softmax(scores, axis=-1).astype(jnp.bfloat16)
    attended = jnp.einsum("phij,jphd->iphd", weights.astype(jnp.float32), value_f)
    return attended.reshape(frames, pixels, channels).astype(jnp.bfloat16)


def general(latents, clip_starts, w_space, w_time, w_qkv, w_out):
    frames, row_count, columns, channels = latents.shape
    device_count = lax.axis_size("frame")
    total_frames = clip_starts.shape[0]
    owned = row_count * columns // device_count
    padded = with_halo(latents, (("slab", 1),), 1)
    hidden = space_conv(padded, w_space)
    full_window = clip_window(clip_starts)
    clip_ids = full_window[2:]
    positions = jnp.arange(total_frames)
    allowed = (positions[None, :] <= positions[:, None]) & (clip_ids[None, :] == clip_ids[:, None])
    payload = hidden.reshape(frames, device_count, owned, channels)
    arrived = lax.all_to_all(payload, "frame", split_axis=1, concat_axis=0, tiled=True)
    pixels = arrived.shape[2]
    extended = jnp.concatenate([jnp.zeros((2, 1, pixels, channels), arrived.dtype), arrived])
    arrived = time_conv(extended, full_window, w_time)
    flattened = arrived.reshape(total_frames, pixels, channels)
    queries, keys_out, values = project(flattened, w_qkv)
    attended = attend(queries, keys_out, values, allowed, HEADS)
    result = jnp.dot(attended.reshape(-1, channels), w_out, preferred_element_type=jnp.float32)
    result = result.astype(jnp.bfloat16).reshape(total_frames, 1, pixels, channels)
    returned = lax.all_to_all(result, "frame", split_axis=0, concat_axis=1, tiled=True)
    returned = returned.reshape(frames, row_count, columns, channels)
    return (latents.astype(jnp.float32) + returned.astype(jnp.float32)).astype(jnp.bfloat16)


def kernel(
    n, slabs, row_count, columns, head_count,
    lat_hbm, starts, ws_hbm, wt_hbm, wqkv_hbm, wo_hbm, out_ref,
    x, ws, wt, wqkv, wo, hid, rx, tx, bias, lag_mask, att,
    load_sem, halo_send, halo_recv, fwd_send, fwd_recv, back_send, back_recv, keep_sem,
):
    frames, pixels, channels = lat_hbm.shape
    total = n * frames
    rows = total * BLOCK
    chunks = pixels // (BLOCK * n)
    blocks = pixels // BLOCK
    first = columns // BLOCK
    me = lax.axis_index("frame")
    slab = lax.axis_index("slab")
    up, down = lax.rem(slab + 1, slabs), lax.rem(slab + slabs - 1, slabs)

    barrier = pltpu.get_barrier_semaphore()
    for step in range(1, n):
        pl.semaphore_signal(
            barrier, inc=1, device_id=(lax.rem(me + step, n), slab), device_id_type=MESH
        )
    for other in (up, down):
        pl.semaphore_signal(barrier, inc=1, device_id=(me, other), device_id_type=MESH)

    pieces = [
        (lat_hbm.at[f], x.at[f, columns : columns + pixels]) for f in range(frames)
    ]
    pieces += [(ws_hbm.at[a, b], ws.at[a, b]) for b in range(3) for a in range(3)]
    early = len(pieces)
    pieces += [(wt_hbm, wt), (wqkv_hbm, wqkv), (wo_hbm, wo)]
    loads = [
        pltpu.make_async_copy(source, target, load_sem.at[i])
        for i, (source, target) in enumerate(pieces)
    ]
    for load in loads[:early]:
        load.start()

    def conv_row(r, waits):
        sums = []
        for b in range(3):
            total_b = None
            for a in range(3):
                if waits:
                    waits.pop(0).wait()
                source = x[:, (r + a) * columns : (r + a + 1) * columns, :]
                part = jnp.dot(
                    source.reshape(frames * columns, channels),
                    ws[a, b],
                    preferred_element_type=jnp.float32,
                )
                total_b = part if total_b is None else total_b + part
            sums.append(total_b)
        place = lax.broadcasted_iota(jnp.int32, (columns, channels), 0)
        for f in range(frames):
            part = [s[f * columns : (f + 1) * columns] for s in sums]
            left = jnp.where(place == 0, 0.0, pltpu.roll(part[0], 1, 0))
            right = jnp.where(place == columns - 1, 0.0, pltpu.roll(part[2], columns - 1, 0))
            v = part[1] + left + right
            hid[f, r * columns : (r + 1) * columns, :] = (
                v / (1.0 + jnp.exp(-v))
            ).astype(jnp.bfloat16)

    def spot(k, owner):
        return pl.multiple_of(lax.rem(first + n * k + owner, blocks) * BLOCK, BLOCK)

    def forward(k, step):
        peer = lax.rem(me + step, n)
        return pltpu.make_async_remote_copy(
            src_ref=hid.at[:, pl.ds(spot(k, peer), BLOCK), :],
            dst_ref=rx.at[k, pl.ds(me * frames, frames)],
            send_sem=fwd_send.at[k, step],
            recv_sem=fwd_recv.at[k, step],
            device_id=(peer, slab),
            device_id_type=MESH,
        )

    def backward(k, step):
        peer = lax.rem(me + step, n)
        return pltpu.make_async_remote_copy(
            src_ref=tx.at[k, pl.ds(peer * frames, frames)],
            dst_ref=out_ref.at[:, pl.ds(spot(k, me), BLOCK), :],
            send_sem=back_send.at[k, step],
            recv_sem=back_recv.at[k, step],
            device_id=(peer, slab),
            device_id_type=MESH,
        )

    def kept(k):
        return pltpu.make_async_copy(
            tx.at[k, pl.ds(me * frames, frames)],
            out_ref.at[:, pl.ds(spot(k, me), BLOCK), :],
            keep_sem.at[k],
        )

    def send_forward(k):
        for step in range(1, n):
            forward(k, step).start()
        rx[k, pl.ds(me * frames, frames)] = hid[:, pl.ds(spot(k, me), BLOCK), :]

    for load in loads[:frames]:
        load.wait()

    halos = [
        pltpu.make_async_remote_copy(
            src_ref=lat_hbm.at[:, pixels - columns : pixels],
            dst_ref=x.at[:, 0:columns],
            send_sem=halo_send.at[0],
            recv_sem=halo_recv.at[0],
            device_id=(me, up),
            device_id_type=MESH,
        ),
        pltpu.make_async_remote_copy(
            src_ref=lat_hbm.at[:, 0:columns],
            dst_ref=x.at[:, columns + pixels : 2 * columns + pixels],
            send_sem=halo_send.at[1],
            recv_sem=halo_recv.at[1],
            device_id=(me, down),
            device_id_type=MESH,
        ),
    ]
    order = list(range(1, row_count)) + [0]
    sent = 0
    waits = loads[frames:early]
    for place, r in enumerate(order):
        if place == row_count - 2:
            for halo in halos:
                halo.wait()

            @pl.when(slab == 0)
            def _():
                x[:, 0:columns] = jnp.zeros((frames, columns, channels), jnp.bfloat16)

            @pl.when(slab == slabs - 1)
            def _():
                x[:, columns + pixels : 2 * columns + pixels] = jnp.zeros(
                    (frames, columns, channels), jnp.bfloat16
                )

        conv_row(r, waits)
        if place == 0:
            pl.semaphore_wait(barrier, n + 1)
            for halo in halos:
                halo.start()
            for load in loads[early:]:
                load.start()
        while (sent + 1) * BLOCK * n <= (place + 1) * columns:
            send_forward(sent)
            sent += 1

    for load in loads[early:]:
        load.wait()

    ids = []
    for f in range(total):
        ids.append(starts[f] if f == 0 else ids[-1] + starts[f])
    row = lax.broadcasted_iota(jnp.int32, (rows, 1), 0)
    col = lax.broadcasted_iota(jnp.int32, (1, rows), 1)
    row_frame, row_pixel = lax.shift_right_logical(row, SHIFT), row & (BLOCK - 1)
    col_frame, col_pixel = lax.shift_right_logical(col, SHIFT), col & (BLOCK - 1)
    row_id, col_id = jnp.zeros_like(row), jnp.zeros_like(col)
    lags = [jnp.zeros((rows, 1), jnp.float32) for _ in range(2)]
    for f in range(total):
        row_id = jnp.where(row_frame == f, ids[f], row_id)
        col_id = jnp.where(col_frame == f, ids[f], col_id)
        for lag in (1, 2):
            if f >= lag:
                same = jnp.where(ids[f - lag] == ids[f], 1.0, 0.0)
                lags[lag - 1] = jnp.where(row_frame == f, same, lags[lag - 1])
    allowed = (row_pixel == col_pixel) & (col_frame <= row_frame) & (row_id == col_id)
    bias[...] = jnp.where(allowed, 0.0, -1e30)
    for lag in range(2):
        lag_mask[lag] = jnp.broadcast_to(lags[lag], (rows, channels)).astype(jnp.bfloat16)

    lanes = 2 * (channels // head_count)
    low = lax.broadcasted_iota(jnp.int32, (rows, lanes), 1) < lanes // 2
    scale = 1.0 / math.sqrt(channels // head_count)

    @pl.loop(0, chunks)
    def _(k):
        for step in range(1, n):
            forward(k, step).wait_recv()
        own = rx[k].reshape(rows, channels)
        mixed = jnp.dot(own, wt[0], preferred_element_type=jnp.float32)
        for lag in (1, 2):
            gap = lag * BLOCK
            lagged = jnp.concatenate(
                [jnp.zeros((gap, channels), jnp.bfloat16), own[: rows - gap]], axis=0
            )
            mixed = mixed + jnp.dot(
                lagged * lag_mask[lag - 1], wt[lag], preferred_element_type=jnp.float32
            )
        mixed = mixed.astype(jnp.bfloat16)
        for pair in range(channels // lanes):
            q, key, value = (
                jnp.dot(
                    mixed,
                    wqkv[:, third * channels + pair * lanes : third * channels + (pair + 1) * lanes],
                    preferred_element_type=jnp.float32,
                ).astype(jnp.bfloat16)
                for third in range(3)
            )
            outs = []
            for half in range(2):
                mine = low if half == 0 else jnp.logical_not(low)
                q_half = jnp.where(mine, q, jnp.zeros_like(q))
                s = lax.dot_general(
                    q_half, key, (((1,), (1,)), ((), ())), preferred_element_type=jnp.float32
                )
                s = s * scale + bias[...]
                e = jnp.exp(s - jnp.max(s, axis=1, keepdims=True))
                norm = jnp.sum(e, axis=1, keepdims=True)
                o = jnp.dot(e.astype(jnp.bfloat16), value, preferred_element_type=jnp.float32)
                outs.append(o / norm)
            att[:, pair * lanes : (pair + 1) * lanes] = jnp.where(low, outs[0], outs[1]).astype(
                jnp.bfloat16
            )
        result = jnp.dot(att[...], wo[...], preferred_element_type=jnp.float32)
        tx[k] = result.astype(jnp.bfloat16).reshape(total, BLOCK, channels)
        for step in range(1, n):
            backward(k, step).start()
        kept(k).start()

    @pl.loop(0, chunks)
    def _(k):
        for step in range(1, n):
            backward(k, step).wait_recv()
        kept(k).wait()

    @pl.loop(0, chunks)
    def _(k):
        for step in range(1, n):
            forward(k, step).wait_send()
            backward(k, step).wait_send()


def fused(latents, clip_starts, w_space, w_time, w_qkv, w_out):
    frames, row_count, columns, channels = latents.shape
    n, slabs = lax.axis_size("frame"), lax.axis_size("slab")
    pixels = row_count * columns
    total = clip_starts.shape[0]
    chunks = pixels // (BLOCK * n)
    rows = total * BLOCK
    bf16 = jnp.bfloat16
    out = pl.pallas_call(
        functools.partial(kernel, n, slabs, row_count, columns, HEADS),
        out_shape=jax.ShapeDtypeStruct((frames, pixels, channels), bf16),
        in_specs=[
            pl.BlockSpec(memory_space=pltpu.HBM),
            pl.BlockSpec(memory_space=pltpu.SMEM),
        ]
        + [pl.BlockSpec(memory_space=pltpu.HBM)] * 4,
        out_specs=pl.BlockSpec(memory_space=pltpu.HBM),
        scratch_shapes=[
            pltpu.VMEM((frames, pixels + 2 * columns, channels), bf16),
            pltpu.VMEM(w_space.shape, bf16),
            pltpu.VMEM(w_time.shape, bf16),
            pltpu.VMEM(w_qkv.shape, bf16),
            pltpu.VMEM(w_out.shape, bf16),
            pltpu.VMEM((frames, pixels, channels), bf16),
            pltpu.VMEM((chunks, total, BLOCK, channels), bf16),
            pltpu.VMEM((chunks, total, BLOCK, channels), bf16),
            pltpu.VMEM((rows, rows), jnp.float32),
            pltpu.VMEM((2, rows, channels), bf16),
            pltpu.VMEM((rows, channels), bf16),
            pltpu.SemaphoreType.DMA((frames + 12,)),
            pltpu.SemaphoreType.DMA((2,)),
            pltpu.SemaphoreType.DMA((2,)),
            pltpu.SemaphoreType.DMA((chunks, n)),
            pltpu.SemaphoreType.DMA((chunks, n)),
            pltpu.SemaphoreType.DMA((chunks, n)),
            pltpu.SemaphoreType.DMA((chunks, n)),
            pltpu.SemaphoreType.DMA((chunks,)),
        ],
        compiler_params=pltpu.CompilerParams(
            collective_id=0, has_side_effects=True, vmem_limit_bytes=54 * 2**20
        ),
    )(latents.reshape(frames, pixels, channels), clip_starts, w_space, w_time, w_qkv, w_out)
    returned = out.reshape(latents.shape)
    return (latents.astype(jnp.float32) + returned.astype(jnp.float32)).astype(bf16)


def on_device(latents, clip_starts, w_space, w_time, w_qkv, w_out):
    frames, row_count, columns, channels = latents.shape
    n, slabs = lax.axis_size("frame"), lax.axis_size("slab")
    fits = (
        (row_count * columns) % (BLOCK * n) == 0
        and columns % BLOCK == 0
        and clip_starts.shape[0] * BLOCK <= 512
        and slabs >= 3
        and row_count >= 3
        and n >= 2
    )
    plan = fused if fits else general
    return plan(latents, clip_starts, w_space, w_time, w_qkv, w_out)


def solution(mesh):
    return jax.shard_map(
        on_device,
        mesh=mesh,
        in_specs=(P("frame", "slab", None, None), P(), P(), P(), P(), P()),
        out_specs=P("frame", "slab", None, None),
        check_vma=False,
    )
```

```python
import functools
import math

import jax
import jax.numpy as jnp
from jax import lax
from jax.experimental import pallas as pl
from jax.experimental.pallas import tpu as pltpu
from jax.sharding import PartitionSpec as P

HEADS = 8
BLOCK = 16
SHIFT = 4
MESH = pl.DeviceIdType.MESH


def with_halo(block, sides, width):
    for axis, dim in sides:
        count = lax.axis_size(axis)
        forward = [(i, i + 1) for i in range(count - 1)]
        backward = [(target, source) for source, target in forward]
        low = lax.ppermute(
            lax.slice_in_dim(block, block.shape[dim] - width, None, axis=dim), axis, forward
        )
        high = lax.ppermute(lax.slice_in_dim(block, 0, width, axis=dim), axis, backward)
        block = jnp.concatenate([low, block, high], axis=dim)
    return block


def space_conv(padded_rows, w_space):
    frames, rows_padded, columns, channels = padded_rows.shape
    row_count = rows_padded - 2
    widened = jnp.pad(padded_rows, ((0, 0), (0, 0), (1, 1), (0, 0)))
    summed = jnp.zeros((frames * row_count * columns, channels), jnp.float32)
    for row_shift in range(3):
        for col_shift in range(3):
            source = widened[
                :, row_shift : row_shift + row_count, col_shift : col_shift + columns
            ].reshape(-1, channels)
            summed = summed + jnp.dot(
                source, w_space[row_shift, col_shift], preferred_element_type=jnp.float32
            )
    return jax.nn.silu(summed).astype(jnp.bfloat16).reshape(frames, row_count, columns, channels)


def clip_window(clip_starts):
    positions = jnp.arange(clip_starts.shape[0])
    upto = positions[None, :] <= positions[:, None]
    clip_ids = jnp.sum(jnp.where(upto, clip_starts[None, :], 0), axis=1)
    return jnp.concatenate([jnp.full((2,), -1, jnp.int32), clip_ids])


def time_conv(extended, window, w_time):
    count = extended.shape[0] - 2
    middle = extended.shape[1:-1]
    channels = extended.shape[-1]
    summed = jnp.zeros((count,) + middle + (channels,), jnp.float32)
    for offset in range(3):
        source = extended[2 - offset : 2 - offset + count].reshape(-1, channels)
        product = jnp.dot(source, w_time[offset], preferred_element_type=jnp.float32).reshape(
            (count,) + middle + (channels,)
        )
        allowed = (window[2 - offset : 2 - offset + count] == window[2:]).astype(jnp.float32)
        summed = summed + product * allowed.reshape((count,) + (1,) * (len(middle) + 1))
    return summed.astype(jnp.bfloat16)


def project(mixed_in, w_qkv):
    frames, pixels, channels = mixed_in.shape
    flattened = jnp.dot(mixed_in.reshape(-1, channels), w_qkv, preferred_element_type=jnp.float32)
    flattened = flattened.astype(jnp.bfloat16).reshape(frames, pixels, 3 * channels)
    return (
        flattened[..., :channels],
        flattened[..., channels : 2 * channels],
        flattened[..., 2 * channels :],
    )


def attend(queries, keys_in, values, allowed, head_count):
    frames, pixels, channels = queries.shape
    head_size = channels // head_count
    query_f = queries.reshape(frames, pixels, head_count, head_size).astype(jnp.float32)
    key_f = keys_in.reshape(frames, pixels, head_count, head_size).astype(jnp.float32)
    value_f = values.reshape(frames, pixels, head_count, head_size).astype(jnp.float32)
    scores = jnp.einsum("iphd,jphd->phij", query_f, key_f) * (1.0 / math.sqrt(head_size))
    scores = jnp.where(allowed, scores, -1e30)
    weights = jax.nn.softmax(scores, axis=-1).astype(jnp.bfloat16)
    attended = jnp.einsum("phij,jphd->iphd", weights.astype(jnp.float32), value_f)
    return attended.reshape(frames, pixels, channels).astype(jnp.bfloat16)


def general(latents, clip_starts, w_space, w_time, w_qkv, w_out):
    frames, row_count, columns, channels = latents.shape
    device_count = lax.axis_size("frame")
    total_frames = clip_starts.shape[0]
    owned = row_count * columns // device_count
    padded = with_halo(latents, (("slab", 1),), 1)
    hidden = space_conv(padded, w_space)
    full_window = clip_window(clip_starts)
    clip_ids = full_window[2:]
    positions = jnp.arange(total_frames)
    allowed = (positions[None, :] <= positions[:, None]) & (clip_ids[None, :] == clip_ids[:, None])
    payload = hidden.reshape(frames, device_count, owned, channels)
    arrived = lax.all_to_all(payload, "frame", split_axis=1, concat_axis=0, tiled=True)
    pixels = arrived.shape[2]
    extended = jnp.concatenate([jnp.zeros((2, 1, pixels, channels), arrived.dtype), arrived])
    arrived = time_conv(extended, full_window, w_time)
    flattened = arrived.reshape(total_frames, pixels, channels)
    queries, keys_out, values = project(flattened, w_qkv)
    attended = attend(queries, keys_out, values, allowed, HEADS)
    result = jnp.dot(attended.reshape(-1, channels), w_out, preferred_element_type=jnp.float32)
    result = result.astype(jnp.bfloat16).reshape(total_frames, 1, pixels, channels)
    returned = lax.all_to_all(result, "frame", split_axis=0, concat_axis=1, tiled=True)
    returned = returned.reshape(frames, row_count, columns, channels)
    return (latents.astype(jnp.float32) + returned.astype(jnp.float32)).astype(jnp.bfloat16)


def kernel(
    n, slabs, row_count, columns, head_count,
    lat_hbm, starts, ws_hbm, wt_hbm, wqkv_hbm, wo_hbm, out_ref,
    x, ws, wt, wqkv, wo, hid, rx, tx, ret, bias, lag_mask, att,
    load_sem, halo_send, halo_recv, fwd_send, fwd_recv, back_send, back_recv,
):
    frames, pixels, channels = lat_hbm.shape
    total = n * frames
    rows = total * BLOCK
    chunks = pixels // (BLOCK * n)
    blocks = pixels // BLOCK
    first = columns // BLOCK
    me = lax.axis_index("frame")
    slab = lax.axis_index("slab")
    up, down = lax.rem(slab + 1, slabs), lax.rem(slab + slabs - 1, slabs)

    barrier = pltpu.get_barrier_semaphore()
    for step in range(1, n):
        pl.semaphore_signal(
            barrier, inc=1, device_id=(lax.rem(me + step, n), slab), device_id_type=MESH
        )
    for other in (up, down):
        pl.semaphore_signal(barrier, inc=1, device_id=(me, other), device_id_type=MESH)

    pieces = [
        (lat_hbm.at[f], x.at[f, columns : columns + pixels]) for f in range(frames)
    ]
    pieces += [(ws_hbm.at[a, b], ws.at[a, b]) for b in range(3) for a in range(3)]
    early = len(pieces)
    pieces += [(wt_hbm, wt), (wqkv_hbm, wqkv), (wo_hbm, wo)]
    loads = [
        pltpu.make_async_copy(source, target, load_sem.at[i])
        for i, (source, target) in enumerate(pieces)
    ]
    for load in loads[:early]:
        load.start()

    def conv_row(r, waits):
        sums = []
        for b in range(3):
            total_b = None
            for a in range(3):
                if waits:
                    waits.pop(0).wait()
                source = x[:, (r + a) * columns : (r + a + 1) * columns, :]
                part = jnp.dot(
                    source.reshape(frames * columns, channels),
                    ws[a, b],
                    preferred_element_type=jnp.float32,
                )
                total_b = part if total_b is None else total_b + part
            sums.append(total_b)
        place = lax.broadcasted_iota(jnp.int32, (columns, channels), 0)
        for f in range(frames):
            part = [s[f * columns : (f + 1) * columns] for s in sums]
            left = jnp.where(place == 0, 0.0, pltpu.roll(part[0], 1, 0))
            right = jnp.where(place == columns - 1, 0.0, pltpu.roll(part[2], columns - 1, 0))
            v = part[1] + left + right
            hid[f, r * columns : (r + 1) * columns, :] = (
                v / (1.0 + jnp.exp(-v))
            ).astype(jnp.bfloat16)

    def spot(k, owner):
        return pl.multiple_of(lax.rem(first + n * k + owner, blocks) * BLOCK, BLOCK)

    def forward(k, step):
        peer = lax.rem(me + step, n)
        return pltpu.make_async_remote_copy(
            src_ref=hid.at[:, pl.ds(spot(k, peer), BLOCK), :],
            dst_ref=rx.at[k, pl.ds(me * frames, frames)],
            send_sem=fwd_send.at[k, step],
            recv_sem=fwd_recv.at[k, step],
            device_id=(peer, slab),
            device_id_type=MESH,
        )

    def backward(k, step):
        peer = lax.rem(me + step, n)
        return pltpu.make_async_remote_copy(
            src_ref=tx.at[k, pl.ds(peer * frames, frames)],
            dst_ref=ret.at[:, pl.ds(spot(k, me), BLOCK), :],
            send_sem=back_send.at[k, step],
            recv_sem=back_recv.at[k, step],
            device_id=(peer, slab),
            device_id_type=MESH,
        )

    def send_forward(k):
        for step in range(1, n):
            forward(k, step).start()
        rx[k, pl.ds(me * frames, frames)] = hid[:, pl.ds(spot(k, me), BLOCK), :]

    for load in loads[:frames]:
        load.wait()

    halos = [
        pltpu.make_async_remote_copy(
            src_ref=lat_hbm.at[:, pixels - columns : pixels],
            dst_ref=x.at[:, 0:columns],
            send_sem=halo_send.at[0],
            recv_sem=halo_recv.at[0],
            device_id=(me, up),
            device_id_type=MESH,
        ),
        pltpu.make_async_remote_copy(
            src_ref=lat_hbm.at[:, 0:columns],
            dst_ref=x.at[:, columns + pixels : 2 * columns + pixels],
            send_sem=halo_send.at[1],
            recv_sem=halo_recv.at[1],
            device_id=(me, down),
            device_id_type=MESH,
        ),
    ]
    order = list(range(1, row_count)) + [0]
    sent = 0
    waits = loads[frames:early]
    for place, r in enumerate(order):
        if place == row_count - 2:
            for halo in halos:
                halo.wait()

            @pl.when(slab == 0)
            def _():
                x[:, 0:columns] = jnp.zeros((frames, columns, channels), jnp.bfloat16)

            @pl.when(slab == slabs - 1)
            def _():
                x[:, columns + pixels : 2 * columns + pixels] = jnp.zeros(
                    (frames, columns, channels), jnp.bfloat16
                )

        conv_row(r, waits)
        if place == 0:
            pl.semaphore_wait(barrier, n + 1)
            for halo in halos:
                halo.start()
            for load in loads[early:]:
                load.start()
        while (sent + 1) * BLOCK * n <= (place + 1) * columns:
            send_forward(sent)
            sent += 1

    for load in loads[early:]:
        load.wait()

    ids = []
    for f in range(total):
        ids.append(starts[f] if f == 0 else ids[-1] + starts[f])
    row = lax.broadcasted_iota(jnp.int32, (rows, 1), 0)
    col = lax.broadcasted_iota(jnp.int32, (1, rows), 1)
    row_frame, row_pixel = lax.shift_right_logical(row, SHIFT), row & (BLOCK - 1)
    col_frame, col_pixel = lax.shift_right_logical(col, SHIFT), col & (BLOCK - 1)
    row_id, col_id = jnp.zeros_like(row), jnp.zeros_like(col)
    lags = [jnp.zeros((rows, 1), jnp.float32) for _ in range(2)]
    for f in range(total):
        row_id = jnp.where(row_frame == f, ids[f], row_id)
        col_id = jnp.where(col_frame == f, ids[f], col_id)
        for lag in (1, 2):
            if f >= lag:
                same = jnp.where(ids[f - lag] == ids[f], 1.0, 0.0)
                lags[lag - 1] = jnp.where(row_frame == f, same, lags[lag - 1])
    allowed = (row_pixel == col_pixel) & (col_frame <= row_frame) & (row_id == col_id)
    bias[...] = jnp.where(allowed, 0.0, -1e30)
    for lag in range(2):
        lag_mask[lag] = jnp.broadcast_to(lags[lag], (rows, channels)).astype(jnp.bfloat16)

    lanes = 2 * (channels // head_count)
    low = lax.broadcasted_iota(jnp.int32, (rows, lanes), 1) < lanes // 2
    scale = 1.0 / math.sqrt(channels // head_count)

    @pl.loop(0, chunks)
    def _(k):
        for step in range(1, n):
            forward(k, step).wait_recv()
        own = rx[k].reshape(rows, channels)
        mixed = jnp.dot(own, wt[0], preferred_element_type=jnp.float32)
        for lag in (1, 2):
            gap = lag * BLOCK
            lagged = jnp.concatenate(
                [jnp.zeros((gap, channels), jnp.bfloat16), own[: rows - gap]], axis=0
            )
            mixed = mixed + jnp.dot(
                lagged * lag_mask[lag - 1], wt[lag], preferred_element_type=jnp.float32
            )
        mixed = mixed.astype(jnp.bfloat16)
        for pair in range(channels // lanes):
            q, key, value = (
                jnp.dot(
                    mixed,
                    wqkv[:, third * channels + pair * lanes : third * channels + (pair + 1) * lanes],
                    preferred_element_type=jnp.float32,
                ).astype(jnp.bfloat16)
                for third in range(3)
            )
            outs = []
            for half in range(2):
                mine = low if half == 0 else jnp.logical_not(low)
                q_half = jnp.where(mine, q, jnp.zeros_like(q))
                s = lax.dot_general(
                    q_half, key, (((1,), (1,)), ((), ())), preferred_element_type=jnp.float32
                )
                s = s * scale + bias[...]
                e = jnp.exp(s - jnp.max(s, axis=1, keepdims=True))
                norm = jnp.sum(e, axis=1, keepdims=True)
                o = jnp.dot(e.astype(jnp.bfloat16), value, preferred_element_type=jnp.float32)
                outs.append(o / norm)
            att[:, pair * lanes : (pair + 1) * lanes] = jnp.where(low, outs[0], outs[1]).astype(
                jnp.bfloat16
            )
        result = jnp.dot(att[...], wo[...], preferred_element_type=jnp.float32)
        tx[k] = result.astype(jnp.bfloat16).reshape(total, BLOCK, channels)
        for step in range(1, n):
            backward(k, step).start()
        ret[:, pl.ds(spot(k, me), BLOCK), :] = tx[k, pl.ds(me * frames, frames)]

    @pl.loop(0, chunks)
    def _(k):
        for step in range(1, n):
            backward(k, step).wait_recv()
        for owner in range(n):
            here = spot(k, owner)
            moved = x[:, pl.ds(here + columns, BLOCK), :].astype(jnp.float32)
            moved = moved + ret[:, pl.ds(here, BLOCK), :].astype(jnp.float32)
            out_ref[:, pl.ds(here, BLOCK), :] = moved.astype(jnp.bfloat16)

    @pl.loop(0, chunks)
    def _(k):
        for step in range(1, n):
            forward(k, step).wait_send()
            backward(k, step).wait_send()


def fused(latents, clip_starts, w_space, w_time, w_qkv, w_out):
    frames, row_count, columns, channels = latents.shape
    n, slabs = lax.axis_size("frame"), lax.axis_size("slab")
    pixels = row_count * columns
    total = clip_starts.shape[0]
    chunks = pixels // (BLOCK * n)
    rows = total * BLOCK
    bf16 = jnp.bfloat16
    hbm = functools.partial(pltpu.with_memory_space_constraint, memory_space=pltpu.HBM)
    out = pl.pallas_call(
        functools.partial(kernel, n, slabs, row_count, columns, HEADS),
        out_shape=jax.ShapeDtypeStruct((frames, pixels, channels), bf16),
        in_specs=[
            pl.BlockSpec(memory_space=pltpu.HBM),
            pl.BlockSpec(memory_space=pltpu.SMEM),
        ]
        + [pl.BlockSpec(memory_space=pltpu.HBM)] * 4,
        out_specs=pl.BlockSpec(memory_space=pltpu.VMEM),
        scratch_shapes=[
            pltpu.VMEM((frames, pixels + 2 * columns, channels), bf16),
            pltpu.VMEM(w_space.shape, bf16),
            pltpu.VMEM(w_time.shape, bf16),
            pltpu.VMEM(w_qkv.shape, bf16),
            pltpu.VMEM(w_out.shape, bf16),
            pltpu.VMEM((frames, pixels, channels), bf16),
            pltpu.VMEM((chunks, total, BLOCK, channels), bf16),
            pltpu.VMEM((chunks, total, BLOCK, channels), bf16),
            pltpu.VMEM((frames, pixels, channels), bf16),
            pltpu.VMEM((rows, rows), jnp.float32),
            pltpu.VMEM((2, rows, channels), bf16),
            pltpu.VMEM((rows, channels), bf16),
            pltpu.SemaphoreType.DMA((frames + 12,)),
            pltpu.SemaphoreType.DMA((2,)),
            pltpu.SemaphoreType.DMA((2,)),
            pltpu.SemaphoreType.DMA((chunks, n)),
            pltpu.SemaphoreType.DMA((chunks, n)),
            pltpu.SemaphoreType.DMA((chunks, n)),
            pltpu.SemaphoreType.DMA((chunks, n)),
        ],
        compiler_params=pltpu.CompilerParams(
            collective_id=0, has_side_effects=True, vmem_limit_bytes=40 * 2**20
        ),
    )(
        hbm(latents.reshape(frames, pixels, channels)),
        hbm(clip_starts),
        *(hbm(weight) for weight in (w_space, w_time, w_qkv, w_out)),
    )
    return out.reshape(latents.shape)


def on_device(latents, clip_starts, w_space, w_time, w_qkv, w_out):
    frames, row_count, columns, channels = latents.shape
    n, slabs = lax.axis_size("frame"), lax.axis_size("slab")
    fits = (
        (row_count * columns) % (BLOCK * n) == 0
        and columns % BLOCK == 0
        and clip_starts.shape[0] * BLOCK <= 512
        and slabs >= 3
        and row_count >= 3
        and n >= 2
    )
    plan = fused if fits else general
    return plan(latents, clip_starts, w_space, w_time, w_qkv, w_out)


def solution(mesh):
    return jax.shard_map(
        on_device,
        mesh=mesh,
        in_specs=(P("frame", "slab", None, None), P(), P(), P(), P(), P()),
        out_specs=P("frame", "slab", None, None),
        check_vma=False,
    )
```
